128 devices in a mesh: row: 8 (over y, core), col: 16 (over z, x).
Axes of the slice: x: 4, y: 4, z: 4, core: 2. Of those that a mesh axis runs over, the one named last changes fastest.
Arguments:
- edge_feats: bfloat16 [262144, 128], P(('row', 'col')), may hold values from -6 to 6
- edge_rows: int32 [262144], P(('row', 'col')), may hold values from 0 to 4095, as said below
- edge_cols: int32 [262144], P(('row', 'col')), may hold values from 0 to 511, as said below
- w_in: bfloat16 [128, 512], replicated, may hold values from -0.5 to 0.5
- w_mid: bfloat16 [512, 512], replicated, may hold values from -0.25 to 0.25
- w_out: bfloat16 [512, 256], replicated, may hold values from -0.25 to 0.25
- cholesky_panel: bfloat16 [65536, 512], P(('row', 'col')), may hold values from -0.375 to 0.375
- diag_inverse: float32 [2, 256, 256], replicated, as said below
Outputs:
- reduced: float32 [65536, 8192], P('row', 'col')
The draws below stay inside these ranges and needn't reach their ends.
Inputs may be any that keep to these rules, and one draw needn't show every extreme that they name: `edge_rows`: on each device the edges are grouped by the device that owns their block: edges d * 16 to (d + 1) * 16 - 1 of a device have their row slot within the row slots of row index d // 16, each row index holding 512 slots in order. `edge_cols`: likewise edges d * 16 to (d + 1) * 16 - 1 have their column slot within the 32 slots of col index d % 16. `diag_inverse`: each block is lower triangular with a positive diagonal.
All inputs are finite; a program needn't handle non-finite values.
Results may differ from the reference program's by a relative error of at most 0.0053.
Values may be sent and summed in bfloat16 or wider, within the bound.
No kernel may reach another device: no remote copies, remote signals or barrier semaphores. Data moves between devices by JAX's collectives and lax.ppermute only.
A program may use at most 448 MiB of HBM per device.

```python
import jax
import jax.numpy as jnp
from jax import lax

ORDER = 65536
TILE = 16
BLOCK = 256
STEPS = 2
FEAT = 128
HIDDEN_UNITS = 512
CAP = 16
WIDTH = 8192
EDGES_DEV = 2048
EDGES = 262144
ROW_SLOTS = 512
COL_SLOTS = 32
N_COL = 16


def edge_bucket():
    index = jnp.arange(EDGES, dtype=jnp.int32)
    return index % EDGES_DEV // CAP


def draw_edge_rows(key, part):
    key = jax.random.fold_in(key, 3)
    owner_row = edge_bucket() // N_COL
    offset = jax.random.randint(key, (EDGES,), 0, ROW_SLOTS, dtype=jnp.int32)
    return (owner_row * ROW_SLOTS + offset).astype(jnp.int32)


def draw_edge_cols(key, part):
    key = jax.random.fold_in(key, 5)
    owner_col = edge_bucket() % N_COL
    offset = jax.random.randint(key, (EDGES,), 0, COL_SLOTS, dtype=jnp.int32)
    return (owner_col * COL_SLOTS + offset).astype(jnp.int32)


def draw_diag_inverse(key, part):
    key = jax.random.fold_in(key, 11)
    key_low, key_diag = jax.random.split(key)
    shape = (STEPS, BLOCK, BLOCK)
    row_index = lax.broadcasted_iota(jnp.int32, shape, 1)
    col_index = lax.broadcasted_iota(jnp.int32, shape, 2)
    lower = jax.random.normal(key_low, shape, jnp.float32) * 0.08
    diagonal = jax.random.uniform(key_diag, shape, jnp.float32, 0.5, 1.5)
    return jnp.where(row_index > col_index, lower, jnp.where(row_index == col_index, diagonal, 0.0)).astype(jnp.float32)


def block_levels(own_key, dims, shards, low, largest):
    level = 1.0
    for axis_at, parts in shards:
        steps = jax.random.uniform(jax.random.fold_in(jax.random.fold_in(own_key, 6), axis_at), (parts,), jnp.float32, low / len(shards), largest / len(shards))
        level = level * jnp.repeat(jnp.exp(steps), dims[axis_at] // parts).reshape((-1,) + (1,) * (len(dims) - 1 - axis_at))
    return level


def centred(stream_key, extent, scale, most, pieces=(), kind=jnp.bfloat16):
    loudness = block_levels(stream_key, extent, pieces, -0.22, 0.18) if pieces else 1.0
    drawn = jax.random.normal(stream_key, extent, jnp.float32) * scale * loudness
    return jnp.minimum(jnp.maximum(drawn, -most), most).astype(kind)


def setup_inputs(seed: int = 0) -> dict:
    arg_keys = jax.random.split(jax.random.key(seed), 9)
    return {
        "edge_feats": centred(arg_keys[0], (EDGES, FEAT), 1.0, 6.0, ((0, 128),)),
        "edge_rows": draw_edge_rows(jax.random.fold_in(arg_keys[8], 71), 0),
        "edge_cols": draw_edge_cols(jax.random.fold_in(arg_keys[8], 71), 0),
        "w_in": centred(arg_keys[3], (FEAT, HIDDEN_UNITS), FEAT ** -0.5, 0.5),
        "w_mid": centred(arg_keys[4], (HIDDEN_UNITS, HIDDEN_UNITS), HIDDEN_UNITS ** -0.5, 0.25),
        "w_out": centred(arg_keys[5], (HIDDEN_UNITS, TILE * TILE), HIDDEN_UNITS ** -0.5, 0.25),
        "cholesky_panel": centred(arg_keys[6], (ORDER, STEPS * BLOCK), BLOCK ** -0.5, 0.375, ((0, 128),)),
        "diag_inverse": draw_diag_inverse(jax.random.fold_in(arg_keys[8], 71), 0),
    }


def edge_network(feats, w_in, w_mid, w_out):
    hidden_one = jax.nn.silu(jnp.dot(feats, w_in, preferred_element_type=jnp.float32)).astype(jnp.bfloat16)
    hidden_two = jax.nn.silu(jnp.dot(hidden_one, w_mid, preferred_element_type=jnp.float32)).astype(jnp.bfloat16)
    return jnp.dot(hidden_two, w_out, preferred_element_type=jnp.float32)


def reference(edge_feats, edge_rows, edge_cols, w_in, w_mid, w_out, cholesky_panel, diag_inverse):
    col_slots = WIDTH // TILE
    total_tiles = (ORDER // TILE) * col_slots
    group_count = EDGES // EDGES_DEV

    def add_group(group, accum):
        start = (group * EDGES_DEV).astype(jnp.int32)
        feats = lax.dynamic_slice_in_dim(edge_feats, start, EDGES_DEV, 0)
        row_slot = lax.dynamic_slice_in_dim(edge_rows, start, EDGES_DEV, 0)
        col_slot = lax.dynamic_slice_in_dim(edge_cols, start, EDGES_DEV, 0)
        target = (row_slot * col_slots + col_slot).astype(jnp.int32)
        return accum.at[target].add(edge_network(feats, w_in, w_mid, w_out))

    accum = jnp.zeros((total_tiles, TILE * TILE), jnp.float32)
    accum = lax.fori_loop(0, group_count, add_group, accum)
    slab = accum.reshape(ORDER // TILE, col_slots, TILE, TILE).transpose(0, 2, 1, 3).reshape(ORDER, WIDTH)
    for block_step in range(STEPS):
        low = block_step * BLOCK
        high = low + BLOCK
        solved = jnp.dot(diag_inverse[block_step], slab[low:high], precision=lax.Precision.HIGHEST,
                         preferred_element_type=jnp.float32)
        solved_b = solved.astype(jnp.bfloat16)
        update = jnp.dot(cholesky_panel[high:, low:high], solved_b, preferred_element_type=jnp.float32)
        slab = jnp.concatenate([slab[:low], solved, slab[high:] - update], axis=0)
    return slab
```

```python
import jax
import jax.numpy as jnp
from jax import lax
from jax.experimental import pallas as pl
from jax.experimental.pallas import tpu as pltpu
from jax.sharding import PartitionSpec as P

TILE = 16
BLOCK = 256
HEAD = 512
LANES = 128
GROUP = 8
CHUNK = 256
SET = 16
PASS = 256
PAYLOAD = 40
MIB = 1024 * 1024
F32 = jnp.float32
BF16 = jnp.bfloat16


def dot(a, b, precision=None):
    return jnp.dot(a, b, precision=precision, preferred_element_type=F32)


def dot_t(a, b):
    return lax.dot_general(a, b, (((1,), (1,)), ((), ())), preferred_element_type=F32)


def silu(v):
    half = 0.5 * v
    return half + half * jnp.tanh(half)


def hidden(feats, w_in, w_mid):
    one = silu(dot(feats, w_in)).astype(BF16)
    return silu(dot(one, w_mid)).astype(BF16)


def iota(shape, dim):
    return lax.broadcasted_iota(jnp.int32, shape, dim)


def head_rows(code_ref, recv_ref, w_in, w_mid, w_tile, head, sums):
    code = code_ref[...]
    slot = code // 32
    column = code % 32
    groups = code.shape[0]
    keep = slot < HEAD // TILE
    ones = jnp.where(keep, 1.0, 0.0).astype(F32)
    upto = jnp.where(iota((LANES, LANES), 0) <= iota((LANES, LANES), 1), 1.0, 0.0).astype(BF16)
    before = jnp.where(iota((groups, groups), 1) < iota((groups, groups), 0), 1.0, 0.0).astype(BF16)
    totals = jnp.broadcast_to(jnp.sum(ones, axis=1, keepdims=True), ones.shape)
    place = dot(ones.astype(BF16), upto) + dot(before, totals.astype(BF16)) - 1.0
    place = jnp.where(keep, place, -1.0)
    count = jnp.sum(ones).astype(jnp.int32)
    slot_f = slot.astype(F32)
    column_f = column.astype(F32)
    sums[...] = jnp.zeros_like(sums)

    def one_pass(step, carry):
        wanted = (iota((PASS, LANES), 0) + step * PASS).astype(F32)
        feats = jnp.zeros((PASS, LANES), F32)
        by_row = jnp.zeros((16, PASS), F32)
        by_col = jnp.zeros((PASS, 16), F32)
        which = iota((16, LANES), 0)
        for g in range(groups):
            pick = jnp.where(place[g : g + 1, :] == wanted, 1.0, 0.0).astype(BF16)
            block = recv_ref[g * 8 : (g + 1) * 8, 16:32, :].reshape(LANES, LANES)
            feats += dot(pick, block)
            where_to = jnp.where(
                which == 0, slot_f[g : g + 1, :], jnp.where(which == 1, column_f[g : g + 1, :], 0.0)
            ).astype(BF16)
            by_row += dot_t(where_to, pick)
            by_col += dot_t(pick, where_to)
        two = hidden(feats.astype(BF16), w_in[...], w_mid[...])
        col_c = by_col[:, 1:2].astype(jnp.int32)
        mask = iota((PASS, 2 * LANES), 1) % LANES // TILE == col_c % GROUP
        row_c = by_row[1:2, :].astype(jnp.int32)
        key = row_c // GROUP * (HEAD // TILE) + by_row[0:1, :].astype(jnp.int32)
        spread = jnp.where(iota((LANES, PASS), 0) == key, 1.0, 0.0).astype(F32)
        for j in range(TILE // 2):
            lanes = slice(j * 2 * LANES, (j + 1) * 2 * LANES)
            values = jnp.where(mask, dot(two, w_tile[:, lanes]), 0.0)
            sums[:, lanes] += dot(spread, values, lax.Precision.HIGHEST)
        return carry

    lax.fori_loop(0, (count + PASS - 1) // PASS, one_pass, 0)
    per = HEAD // TILE
    for a in range(TILE):
        for q in range(HEAD // LANES):
            head[pl.ds(q * HEAD + a, per, stride=TILE), :] = sums[
                q * per : (q + 1) * per, a * LANES : (a + 1) * LANES
            ]


def some(bits):
    return bits != 0


def low_bit(bits):
    low = bits & -bits
    place = 0
    for width, mask in ((8, 0xFF00), (4, 0xF0F0), (2, 0xCCCC), (1, 0xAAAA)):
        place = place + jnp.where((low & mask) != 0, width, 0)
    return place


def assemble_kernel(dest, lost, clashes, code_ref, recv_ref, lane_ref, w_in, w_mid, w_tile, slab, head, tiles, sums):
    peers = CHUNK // SET

    def clear(i, carry):
        slab[pl.ds(pl.multiple_of(i * 512, 512), 512), :] = jnp.zeros((512, LANES), F32)
        return carry

    lax.fori_loop(0, slab.shape[0] // 512, clear, 0)

    def chunk(k, carry):
        start = pl.multiple_of(k * peers, peers)
        feats = recv_ref[pl.ds(start, peers), 0:16, :].reshape(CHUNK, LANES)
        two = hidden(feats, w_in[...], w_mid[...])
        lane = lane_ref[pl.ds(start, peers), :]
        lane = jnp.broadcast_to(lane[:, None, :], (peers, 16, 16)).reshape(CHUNK, 16)
        own = iota((CHUNK, 16), 0) % 16 == iota((CHUNK, 16), 1)
        lane = jnp.sum(jnp.where(own, lane, 0.0), axis=1, keepdims=True).astype(jnp.int32)
        mask = iota((CHUNK, LANES), 1) // TILE == lane
        for j in range(TILE // 2):
            pair = dot(two, w_tile[:, j * 2 * LANES : (j + 1) * 2 * LANES])
            for i in range(2):
                tiles[pl.ds(2 * j + i, CHUNK, stride=TILE), :] = jnp.where(
                    mask, pair[:, i * LANES : (i + 1) * LANES], 0.0
                )

        def load(e):
            return tiles[pl.ds(pl.multiple_of(e * TILE, TILE), TILE), :]

        def place(i, inner):
            at = [pl.multiple_of(dest[k * CHUNK + i * SET + e], TILE) for e in range(SET)]
            sums = [slab[pl.ds(at[e], TILE), :] + load(i * SET + e) for e in range(SET)]
            for e in range(SET):
                slab[pl.ds(at[e], TILE), :] = sums[e]
            return inner

        def repair(bits):
            peer = low_bit(bits)

            def one(left):
                e = peer * SET + low_bit(left)
                at = pl.multiple_of(dest[k * CHUNK + e], TILE)
                slab[pl.ds(at, TILE), :] += load(e)
                return left & (left - 1)

            lax.while_loop(some, one, lost[k * peers + peer])
            return bits & (bits - 1)

        lax.fori_loop(0, CHUNK // SET, place, 0)
        lax.while_loop(some, repair, clashes[k])
        return carry

    lax.fori_loop(0, recv_ref.shape[0] // peers, chunk, 0)
    head_rows(code_ref, recv_ref, w_in, w_mid, w_tile, head, sums)


def solve(head, dinv, corner, solved, solved_b):
    quarters = [head[q * HEAD : (q + 1) * HEAD, :] for q in range(HEAD // LANES)]
    rows = jnp.concatenate(quarters, axis=1)
    top = dot(dinv[0], rows[:BLOCK, :], lax.Precision.HIGHEST)
    top_b = top.astype(BF16)
    solved[:BLOCK, :] = top
    solved_b[:BLOCK, :] = top_b
    lost = dot(corner[:BLOCK, :], top_b[:LANES, :]) + dot(corner[BLOCK:, :], top_b[LANES:, :])
    rest = rows[BLOCK:, :] - lost
    low = dot(dinv[1], rest, lax.Precision.HIGHEST)
    solved[BLOCK:, :] = low
    solved_b[BLOCK:, :] = low.astype(BF16)


def update_kernel(
    first, panel_any, head, dinv, corner, slab, out, panel, result, solved_b, solved, in_sems, out_sems
):
    count = in_sems.shape[0]
    total = out.shape[0]
    rows = total // count

    def here(i):
        return pl.ds(pl.multiple_of(i * rows, rows), rows)

    def fetch(i):
        return pltpu.make_async_copy(panel_any.at[here(i), :], panel.at[here(i), :], in_sems.at[i])

    def give(i):
        return pltpu.make_async_copy(result.at[here(i), :], out.at[here(i), :], out_sems.at[i])

    for i in range(count):
        fetch(i).start()

    solve(head, dinv, corner, solved, solved_b)

    def step(i, carry):
        fetch(i).wait()
        for j in range(HEAD // (2 * LANES)):
            lost = dot(panel[here(i), :], solved_b[:, j * 2 * LANES : (j + 1) * 2 * LANES])
            for q in (2 * j, 2 * j + 1):
                start = pl.multiple_of(q * total + i * rows, rows)
                part = lost[:, (q - 2 * j) * LANES : (q - 2 * j + 1) * LANES]
                result[here(i), q * LANES : (q + 1) * LANES] = slab[pl.ds(start, rows), :] - part

        @pl.when(jnp.logical_and(first[0] == 1, i == 0))
        def _():
            result[:HEAD, :] = solved[...]

        give(i).start()
        return carry

    lax.fori_loop(0, count, step, 0)

    def finish(i, carry):
        give(i).wait()
        return carry

    lax.fori_loop(0, count, finish, 0)


def vmem():
    return pl.BlockSpec(memory_space=pltpu.VMEM)


def body(edge_feats, edge_rows, edge_cols, w_in, w_mid, w_out, cholesky_panel, diag_inverse):
    n_row = lax.axis_size("row")
    n_col = lax.axis_size("col")
    peers = n_row * n_col
    rows_dev = cholesky_panel.shape[0] * n_col
    slots = rows_dev // TILE
    panel = lax.all_gather(cholesky_panel, "col", axis=0, tiled=True)
    corner = cholesky_panel[BLOCK : 2 * BLOCK, :BLOCK]
    corner = jnp.concatenate([corner[:, :LANES], corner[:, LANES:]], axis=0).reshape(peers, 4, LANES)

    feats = edge_feats.reshape(peers, 16, LANES)
    row = (edge_rows % slots).reshape(peers, 16)
    col = (edge_cols % 32).reshape(peers, 16)
    place = jnp.concatenate([row // 32, row % 32, col], axis=1)
    both = jnp.concatenate(
        [place, jnp.tile(place[:n_col], (n_row, 1)), jnp.zeros((peers, 32), jnp.int32)], axis=1
    ).astype(BF16)
    payload = jnp.concatenate(
        [
            feats,
            jnp.tile(feats[:n_col], (n_row, 1, 1)),
            both[:, None, :],
            corner,
            jnp.zeros((peers, PAYLOAD - 37, LANES), BF16),
        ],
        axis=1,
    )
    recv = lax.all_to_all(payload, ("row", "col"), 0, 0, tiled=True)
    corner = jnp.broadcast_to(recv[:1, 33:37, :], (peers, 4, LANES))
    corner = lax.all_to_all(corner, ("row", "col"), 0, 0, tiled=True).reshape(2 * BLOCK, LANES)
    info = recv[:, 32, :96].astype(jnp.int32)
    own_row = info[:, 0:16] * 32 + info[:, 16:32]
    own_col = info[:, 32:48]
    window = own_col // GROUP * rows_dev + own_row * TILE
    dest = window.reshape(-1)
    later = iota((SET, SET), 1) > iota((SET, SET), 0)
    same = (window[:, :, None] == window[:, None, :]) & later
    bit = 1 << jnp.arange(16, dtype=jnp.int32)
    lost = jnp.sum(jnp.where(jnp.any(same, axis=2), bit, 0), axis=1)
    clashes = jnp.sum(jnp.where(lost.reshape(-1, CHUNK // SET) != 0, bit, 0), axis=1)
    lane = (own_col % GROUP).astype(F32)
    code = ((info[:, 48:64] * 32 + info[:, 64:80]) * 32 + info[:, 80:96]).reshape(-1, LANES)

    source = iota((256, 16 * LANES), 0)
    target = iota((256, 16 * LANES), 1)
    repeat = (source == target // LANES * TILE + target % TILE).astype(BF16)
    w_tile = dot(w_out, repeat).astype(BF16)

    slab, head = pl.pallas_call(
        assemble_kernel,
        out_shape=(
            pltpu.VMEM((rows_dev * HEAD // LANES, LANES), F32),
            pltpu.VMEM((HEAD * HEAD // LANES, LANES), F32),
        ),
        in_specs=[pl.BlockSpec(memory_space=pltpu.SMEM)] * 3 + [vmem()] * 6,
        out_specs=(vmem(), vmem()),
        scratch_shapes=[pltpu.VMEM((CHUNK * TILE, LANES), F32), pltpu.VMEM((LANES, 16 * LANES), F32)],
        compiler_params=pltpu.CompilerParams(vmem_limit_bytes=26 * MIB),
        cost_estimate=pl.CostEstimate(flops=15_000_000_000, bytes_accessed=24_000_000, transcendentals=0),
    )(dest, lost, clashes, code, recv, lane, w_in, w_mid, w_tile)

    first = (lax.axis_index("row") == 0).astype(jnp.int32).reshape(1)
    anywhere = pl.BlockSpec(memory_space=pl.ANY)
    return pl.pallas_call(
        update_kernel,
        out_shape=jax.ShapeDtypeStruct((rows_dev, HEAD), F32),
        in_specs=[pl.BlockSpec(memory_space=pltpu.SMEM), anywhere] + [vmem()] * 4,
        out_specs=anywhere,
        scratch_shapes=[
            pltpu.VMEM((rows_dev, HEAD), BF16),
            pltpu.VMEM((rows_dev, HEAD), F32),
            pltpu.VMEM((HEAD, HEAD), BF16),
            pltpu.VMEM((HEAD, HEAD), F32),
            pltpu.SemaphoreType.DMA((8,)),
            pltpu.SemaphoreType.DMA((8,)),
        ],
        compiler_params=pltpu.CompilerParams(vmem_limit_bytes=30 * MIB),
        cost_estimate=pl.CostEstimate(flops=4_300_000_000, bytes_accessed=42_000_000, transcendentals=0),
    )(
        first,
        pltpu.with_memory_space_constraint(panel, pltpu.HBM),
        pltpu.with_memory_space_constraint(head, pltpu.VMEM),
        diag_inverse,
        corner,
        pltpu.with_memory_space_constraint(slab, pltpu.VMEM),
    )


def solution(mesh):
    return jax.shard_map(
        body,
        mesh=mesh,
        in_specs=(
            P(("row", "col"), None),
            P(("row", "col")),
            P(("row", "col")),
            P(),
            P(),
            P(),
            P(("row", "col"), None),
            P(),
        ),
        out_specs=P("row", "col"),
        check_vma=False,
    )
```

```python
import functools

import jax
import jax.numpy as jnp
from jax import lax
from jax.experimental import pallas as pl
from jax.experimental.pallas import tpu as pltpu
from jax.sharding import PartitionSpec as P

TILE = 16
BLOCK = 256
HEAD = 512
LANES = 128
GROUP = 8
CHUNK = 256
HIDDEN = 512
SET = 16
PASS = 256
PAYLOAD = 40
MIB = 1024 * 1024
F32 = jnp.float32
BF16 = jnp.bfloat16


def dot(a, b, precision=None):
    return jnp.dot(a, b, precision=precision, preferred_element_type=F32)


def dot_t(a, b):
    return lax.dot_general(a, b, (((1,), (1,)), ((), ())), preferred_element_type=F32)


def silu(v):
    half = 0.5 * v
    return half + half * jnp.tanh(half)


def hidden(feats, w_in, w_mid):
    one = silu(dot(feats, w_in)).astype(BF16)
    return silu(dot(one, w_mid)).astype(BF16)


def iota(shape, dim):
    return lax.broadcasted_iota(jnp.int32, shape, dim)


def head_rows(code_ref, recv_ref, w_in, w_mid, w_tile, head, sums):
    code = code_ref[...]
    slot = code // 32
    column = code % 32
    groups = code.shape[0]
    keep = slot < HEAD // TILE
    ones = jnp.where(keep, 1.0, 0.0).astype(F32)
    upto = jnp.where(iota((LANES, LANES), 0) <= iota((LANES, LANES), 1), 1.0, 0.0).astype(BF16)
    before = jnp.where(iota((groups, groups), 1) < iota((groups, groups), 0), 1.0, 0.0).astype(BF16)
    totals = jnp.broadcast_to(jnp.sum(ones, axis=1, keepdims=True), ones.shape)
    place = dot(ones.astype(BF16), upto) + dot(before, totals.astype(BF16)) - 1.0
    place = jnp.where(keep, place, -1.0)
    count = jnp.sum(ones).astype(jnp.int32)
    slot_f = slot.astype(F32)
    column_f = column.astype(F32)
    sums[...] = jnp.zeros_like(sums)

    def one_pass(step, carry):
        wanted = (iota((PASS, LANES), 0) + step * PASS).astype(F32)
        feats = jnp.zeros((PASS, LANES), F32)
        by_row = jnp.zeros((16, PASS), F32)
        by_col = jnp.zeros((PASS, 16), F32)
        which = iota((16, LANES), 0)
        for g in range(groups):
            pick = jnp.where(place[g : g + 1, :] == wanted, 1.0, 0.0).astype(BF16)
            block = recv_ref[g * 8 : (g + 1) * 8, 16:32, :].reshape(LANES, LANES)
            feats += dot(pick, block)
            where_to = jnp.where(
                which == 0, slot_f[g : g + 1, :], jnp.where(which == 1, column_f[g : g + 1, :], 0.0)
            ).astype(BF16)
            by_row += dot_t(where_to, pick)
            by_col += dot_t(pick, where_to)
        two = hidden(feats.astype(BF16), w_in[...], w_mid[...])
        col_c = by_col[:, 1:2].astype(jnp.int32)
        mask = iota((PASS, 2 * LANES), 1) % LANES // TILE == col_c % GROUP
        row_c = by_row[1:2, :].astype(jnp.int32)
        key = row_c // GROUP * (HEAD // TILE) + by_row[0:1, :].astype(jnp.int32)
        spread = jnp.where(iota((LANES, PASS), 0) == key, 1.0, 0.0).astype(F32)
        for j in range(TILE // 2):
            lanes = slice(j * 2 * LANES, (j + 1) * 2 * LANES)
            values = jnp.where(mask, dot(two, w_tile[:, lanes]), 0.0)
            sums[:, lanes] += dot(spread, values, lax.Precision.HIGHEST)
        return carry

    lax.fori_loop(0, (count + PASS - 1) // PASS, one_pass, 0)
    per = HEAD // TILE
    for a in range(TILE):
        for q in range(HEAD // LANES):
            head[pl.ds(q * HEAD + a, per, stride=TILE), :] = sums[
                q * per : (q + 1) * per, a * LANES : (a + 1) * LANES
            ]


def solve(head, dinv, corner, solved, solved_b):
    quarters = [head[q * HEAD : (q + 1) * HEAD, :] for q in range(HEAD // LANES)]
    rows = jnp.concatenate(quarters, axis=1)
    top = dot(dinv[0], rows[:BLOCK, :], lax.Precision.HIGHEST)
    top_b = top.astype(BF16)
    solved[:BLOCK, :] = top
    solved_b[:BLOCK, :] = top_b
    lost = dot(corner[:BLOCK, :], top_b[:LANES, :]) + dot(corner[BLOCK:, :], top_b[LANES:, :])
    rest = rows[BLOCK:, :] - lost
    low = dot(dinv[1], rest, lax.Precision.HIGHEST)
    solved[BLOCK:, :] = low
    solved_b[BLOCK:, :] = low.astype(BF16)


def some(bits):
    return bits != 0


def low_bit(bits):
    low = bits & -bits
    place = 0
    for width, mask in ((8, 0xFF00), (4, 0xF0F0), (2, 0xCCCC), (1, 0xAAAA)):
        place = place + jnp.where((low & mask) != 0, width, 0)
    return place


def hidden_kernel(code, recv, w_in, w_mid, w_tile, two, head, sums):
    def chunk(k, carry):
        peers = HIDDEN // SET
        feats = recv[pl.ds(pl.multiple_of(k * peers, peers), peers), 0:16, :].reshape(HIDDEN, LANES)
        two[pl.ds(pl.multiple_of(k * HIDDEN, HIDDEN), HIDDEN), :] = hidden(feats, w_in[...], w_mid[...])
        return carry

    head_rows(code, recv, w_in, w_mid, w_tile, head, sums)
    lax.fori_loop(0, two.shape[0] // HIDDEN, chunk, 0)


def assemble(dest, lost, clashes, two, lane_ref, w_tile, slab, tiles, early):
    peers = CHUNK // SET

    def clear(i, carry):
        slab[pl.ds(pl.multiple_of(i * 512, 512), 512), :] = jnp.zeros((512, LANES), F32)
        return carry

    lax.fori_loop(0, slab.shape[0] // 512, clear, 0)
    for copy in early:
        copy.wait()

    def chunk(k, carry):
        start = pl.multiple_of(k * peers, peers)
        rows = two[pl.ds(pl.multiple_of(k * CHUNK, CHUNK), CHUNK), :]
        lane = lane_ref[pl.ds(start, peers), :]
        lane = jnp.broadcast_to(lane[:, None, :], (peers, 16, 16)).reshape(CHUNK, 16)
        own = iota((CHUNK, 16), 0) % 16 == iota((CHUNK, 16), 1)
        lane = jnp.sum(jnp.where(own, lane, 0.0), axis=1, keepdims=True).astype(jnp.int32)
        mask = iota((CHUNK, LANES), 1) // TILE == lane
        for j in range(TILE // 2):
            pair = dot(rows, w_tile[:, j * 2 * LANES : (j + 1) * 2 * LANES])
            for i in range(2):
                tiles[pl.ds(2 * j + i, CHUNK, stride=TILE), :] = jnp.where(
                    mask, pair[:, i * LANES : (i + 1) * LANES], 0.0
                )

        def load(e):
            return tiles[pl.ds(pl.multiple_of(e * TILE, TILE), TILE), :]

        def place(i, inner):
            at = [pl.multiple_of(dest[k * CHUNK + i * SET + e], TILE) for e in range(SET)]
            sums = [slab[pl.ds(at[e], TILE), :] + load(i * SET + e) for e in range(SET)]
            for e in range(SET):
                slab[pl.ds(at[e], TILE), :] = sums[e]
            return inner

        def repair(bits):
            peer = low_bit(bits)

            def one(left):
                e = peer * SET + low_bit(left)
                at = pl.multiple_of(dest[k * CHUNK + e], TILE)
                slab[pl.ds(at, TILE), :] += load(e)
                return left & (left - 1)

            lax.while_loop(some, one, lost[k * peers + peer])
            return bits & (bits - 1)

        lax.fori_loop(0, CHUNK // SET, place, 0)
        lax.while_loop(some, repair, clashes[k])
        return carry

    lax.fori_loop(0, two.shape[0] // CHUNK, chunk, 0)


def final_kernel(count, *refs):
    place, dest, lost, clashes, two, lane, w_tile, head, dinv, corner = refs[:10]
    pieces = refs[10 : 10 + count]
    out, solved_b = refs[10 + count : 12 + count]
    slab, tiles, solved, panel, result, two_v, tile_v, in_sems, out_sems, sems = refs[12 + count :]
    total = out.shape[0]
    blocks = out_sems.shape[0]
    rows = total // blocks
    copies = [pltpu.make_async_copy(piece, panel.at[i], in_sems.at[i]) for i, piece in enumerate(pieces)]
    early = [pltpu.make_async_copy(two, two_v, sems.at[0]), pltpu.make_async_copy(w_tile, tile_v, sems.at[1])]
    for copy in early + copies:
        copy.start()
    solve(head, dinv, corner, solved, solved_b)
    assemble(dest, lost, clashes, two_v, lane, tile_v, slab, tiles, early)
    for copy in copies:
        copy.wait()

    def block(i):
        return pl.ds(pl.multiple_of(i * rows, rows), rows)

    def give(i):
        return pltpu.make_async_copy(result.at[block(i), :], out.at[block(place[i]), :], out_sems.at[i])

    def part(i, q):
        return slab[pl.ds(pl.multiple_of(q * total + place[i] * rows, rows), rows), :]

    def leave(i):
        @pl.when(jnp.logical_and(place[blocks] == 1, place[i] == 0))
        def _():
            result[block(i), :] = solved[...]

        give(i).start()

    def step(i, carry):
        for j in range(HEAD // (2 * LANES)):
            less = dot(panel[i], solved_b[:, j * 2 * LANES : (j + 1) * 2 * LANES])
            for q in (2 * j, 2 * j + 1):
                lanes = slice((q - 2 * j) * LANES, (q - 2 * j + 1) * LANES)
                result[block(i), q * LANES : (q + 1) * LANES] = part(i, q) - less[:, lanes]
        leave(i)
        return carry

    def plain(i, carry):
        for q in range(HEAD // LANES):
            result[block(i), q * LANES : (q + 1) * LANES] = part(i, q)
        leave(i)
        return carry

    lax.fori_loop(count, blocks, plain, 0)
    lax.fori_loop(0, count, step, 0)

    def finish(i, carry):
        give(i).wait()
        return carry

    lax.fori_loop(0, blocks, finish, 0)


def last_kernel(first, *refs):
    place, solved_b, before = refs[:3]
    count = place.shape[0] - 1 - first
    pieces = refs[3 : 3 + count]
    out, panel, result, in_sems, take_sems, out_sems = refs[3 + count :]
    rows = pieces[0].shape[0]

    def block(i):
        return pl.ds(pl.multiple_of(place[first + i] * rows, rows), rows)

    fetches = [pltpu.make_async_copy(pieces[i], panel.at[i], in_sems.at[i]) for i in range(count)]
    takes = [pltpu.make_async_copy(before.at[block(i), :], result.at[i], take_sems.at[i]) for i in range(count)]
    gives = [pltpu.make_async_copy(result.at[i], out.at[block(i), :], out_sems.at[i]) for i in range(count)]
    for copy in fetches + takes:
        copy.start()
    for i in range(count):
        fetches[i].wait()
        takes[i].wait()

        @pl.when(jnp.logical_not(jnp.logical_and(place[first + count] == 1, place[first + i] == 0)))
        def _():
            for j in range(HEAD // (2 * LANES)):
                lanes = slice(j * 2 * LANES, (j + 1) * 2 * LANES)
                result[i, :, lanes] -= dot(panel[i], solved_b[:, lanes])

        gives[i].start()
    for copy in gives:
        copy.wait()


def vmem():
    return pl.BlockSpec(memory_space=pltpu.VMEM)


def payload_kernel(feats, rows, cols, corner, out):
    peers = feats.shape[0]
    n_col = 16
    groups, per = rows.shape[0], peers // rows.shape[0]
    code = (rows[...] & 511) * 32 + (cols[...] & 31)
    high, low = (code >> 7).astype(F32), (code & 127).astype(F32)
    line = iota((8, LANES), 0)
    out[:, 0:16, :] = feats[...]
    for i in range(peers // n_col):
        out[i * n_col : (i + 1) * n_col, 16:32, :] = feats[:n_col, :, :]
    for g in range(groups):
        h = g % (n_col // per)
        block = jnp.where(line == 0, high[g : g + 1, :], low[g : g + 1, :])
        block = jnp.where(line == 2, high[h : h + 1, :], jnp.where(line == 3, low[h : h + 1, :], block))
        block = jnp.broadcast_to(block[None], (per, 8, LANES))
        slices = corner[g * per : (g + 1) * per, :, :].astype(F32)
        out[g * per : (g + 1) * per, 32:40, :] = jnp.where(line[None] < 4, block, slices).astype(BF16)


def along_x(value, by):
    return lax.ppermute(value, "col", [(z * 4 + x, z * 4 + (x + by) % 4) for z in range(4) for x in range(4)])


def along_z(value, by):
    return lax.ppermute(value, "col", [(z * 4 + x, (z + by) % 4 * 4 + x) for z in range(4) for x in range(4)])


def start_gather(own):
    got = {"own": own}
    got["left"], got["right"] = along_x(own, 1), along_x(own, -1)
    got["down"], got["up"] = along_z(own, 1), along_z(own, -1)
    return got


def together(got, *others):
    values = lax.optimization_barrier((*got.values(), *others))
    return dict(zip(got, values[: len(got)], strict=True)), *values[len(got) :]


def second_gather(near):
    got = {(0, 0): near["own"], (-1, 0): near["left"], (1, 0): near["right"], (0, -1): near["down"], (0, 1): near["up"]}
    got[1, 1] = along_x(got[0, 1], -1)
    got[1, -1] = along_z(got[1, 0], 1)
    got[-1, 1] = along_z(got[-1, 0], -1)
    got[-1, -1] = along_x(got[0, -1], 1)
    return got


def third_gather(got):
    got[2, 1] = along_x(got[1, 1], -1)
    got[-1, 2] = along_z(got[-1, 1], -1)
    got[2, 0] = along_x(got[-1, 0], 1)
    got[0, 2] = along_z(got[0, -1], 1)
    return got


def fourth_gather(got):
    got[2, -1] = along_x(got[1, -1], -1)
    got[1, 2] = along_z(got[1, 1], -1)
    got[2, 2] = along_x(got[-1, 2], 1)
    return got


def body(edge_feats, edge_rows, edge_cols, w_in, w_mid, w_out, cholesky_panel, diag_inverse):
    n_row = lax.axis_size("row")
    n_col = lax.axis_size("col")
    peers = n_row * n_col
    rows_dev = cholesky_panel.shape[0] * n_col
    slots = rows_dev // TILE
    got = start_gather(cholesky_panel)
    corner = cholesky_panel[BLOCK : 2 * BLOCK, :BLOCK]
    corner = jnp.concatenate([corner[:, :LANES], corner[:, LANES:]], axis=0).reshape(peers, 4, LANES)
    corner = jnp.pad(corner, ((0, 0), (4, 0), (0, 0)))

    feats = edge_feats.reshape(peers, 16, LANES)
    payload = pl.pallas_call(
        payload_kernel,
        out_shape=jax.ShapeDtypeStruct((peers, PAYLOAD, LANES), BF16),
        in_specs=[vmem()] * 4,
        out_specs=vmem(),
        compiler_params=pltpu.CompilerParams(vmem_limit_bytes=16 * MIB),
    )(feats, edge_rows.reshape(16, LANES), edge_cols.reshape(16, LANES), corner)
    payload, got = lax.optimization_barrier((payload, got))
    recv = lax.all_to_all(payload, ("row", "col"), 0, 0, tiled=True)
    corner = jnp.broadcast_to(recv[:1, 36:40, :], (peers, 4, LANES))
    corner = lax.all_to_all(corner, ("row", "col"), 0, 0, tiled=True).reshape(2 * BLOCK, LANES)
    own_lane = lax.axis_index("col") % GROUP * 16
    info = lax.dynamic_slice(recv, (0, 32, own_lane), (peers, 4, 16)).astype(jnp.int32)
    own = info[:, 0, :] * 128 + info[:, 1, :]
    own_row, own_col = own // 32, own % 32
    window = own_col // GROUP * rows_dev + own_row * TILE
    dest = window.reshape(-1)
    code = (info[:, 2, :] * 128 + info[:, 3, :]).reshape(-1, LANES)
    later = iota((SET, SET), 1) > iota((SET, SET), 0)
    same = (window[:, :, None] == window[:, None, :]) & later
    bit = 1 << jnp.arange(16, dtype=jnp.int32)
    lost = jnp.sum(jnp.where(jnp.any(same, axis=2), bit, 0), axis=1)
    clashes = jnp.sum(jnp.where(lost.reshape(-1, CHUNK // SET) != 0, bit, 0), axis=1)
    lane = (own_col % GROUP).astype(F32)

    source = iota((256, 16 * LANES), 0)
    target = iota((256, 16 * LANES), 1)
    repeat = (source == target // LANES * TILE + target % TILE).astype(BF16)
    w_tile = dot(w_out, repeat).astype(BF16)

    anywhere = pl.BlockSpec(memory_space=pl.ANY)
    smem = pl.BlockSpec(memory_space=pltpu.SMEM)
    got, recv = together(second_gather(got), recv)
    got = third_gather(got)
    two, head = pl.pallas_call(
        hidden_kernel,
        out_shape=(
            jax.ShapeDtypeStruct((16 * peers, w_mid.shape[1]), BF16),
            jax.ShapeDtypeStruct((HEAD * HEAD // LANES, LANES), F32),
        ),
        in_specs=[vmem()] * 5,
        out_specs=(vmem(), vmem()),
        scratch_shapes=[pltpu.VMEM((LANES, 16 * LANES), F32)],
        compiler_params=pltpu.CompilerParams(vmem_limit_bytes=20 * MIB),
        cost_estimate=pl.CostEstimate(flops=10_000_000_000, bytes_accessed=8_000_000, transcendentals=0),
    )(code, recv, w_in, w_mid, w_tile)
    got, two, head = together(got, two, head)
    ready = len(got)
    got = fourth_gather(got)
    me = lax.axis_index("col")
    x, z = me % 4, me // 4
    place = [(z + dz) % 4 * 4 + (x + dx) % 4 for dx, dz in got]
    place = jnp.stack(place + [(lax.axis_index("row") == 0).astype(jnp.int32)]).astype(jnp.int32)
    count = len(got)
    pieces = list(got.values())
    held = [pltpu.with_memory_space_constraint(value, pltpu.HBM) for value in pieces[:ready]]
    part, solved_b = pl.pallas_call(
        functools.partial(final_kernel, ready),
        out_shape=(
            jax.ShapeDtypeStruct((rows_dev, HEAD), F32),
            jax.ShapeDtypeStruct((HEAD, HEAD), BF16),
        ),
        in_specs=[smem] * 4 + [anywhere, vmem(), anywhere] + [vmem()] * 3 + [anywhere] * ready,
        out_specs=(anywhere, vmem()),
        scratch_shapes=[
            pltpu.VMEM((rows_dev * HEAD // LANES, LANES), F32),
            pltpu.VMEM((CHUNK * TILE, LANES), F32),
            pltpu.VMEM((HEAD, HEAD), F32),
            pltpu.VMEM((ready, *cholesky_panel.shape), BF16),
            pltpu.VMEM((rows_dev, HEAD), F32),
            pltpu.VMEM(two.shape, BF16),
            pltpu.VMEM(w_tile.shape, BF16),
            pltpu.SemaphoreType.DMA((ready,)),
            pltpu.SemaphoreType.DMA((count,)),
            pltpu.SemaphoreType.DMA((2,)),
        ],
        compiler_params=pltpu.CompilerParams(vmem_limit_bytes=56 * MIB),
        cost_estimate=pl.CostEstimate(flops=15_000_000_000, bytes_accessed=30_000_000, transcendentals=0),
    )(place, dest, lost, clashes, two, lane, w_tile, head, diag_inverse, corner, *held)
    left = count - ready
    return pl.pallas_call(
        functools.partial(last_kernel, ready),
        out_shape=jax.ShapeDtypeStruct((rows_dev, HEAD), F32),
        in_specs=[smem, vmem()] + [anywhere] * (1 + left),
        out_specs=anywhere,
        scratch_shapes=[
            pltpu.VMEM((left, *cholesky_panel.shape), BF16),
            pltpu.VMEM((left, cholesky_panel.shape[0], HEAD), F32),
            pltpu.SemaphoreType.DMA((left,)),
            pltpu.SemaphoreType.DMA((left,)),
            pltpu.SemaphoreType.DMA((left,)),
        ],
        input_output_aliases={2: 0},
        compiler_params=pltpu.CompilerParams(vmem_limit_bytes=16 * MIB),
        cost_estimate=pl.CostEstimate(flops=800_000_000, bytes_accessed=8_000_000, transcendentals=0),
    )(place, solved_b, part, *pieces[ready:])


def solution(mesh):
    return jax.shard_map(
        body,
        mesh=mesh,
        in_specs=(
            P(("row", "col"), None),
            P(("row", "col")),
            P(("row", "col")),
            P(),
            P(),
            P(),
            P(("row", "col"), None),
            P(),
        ),
        out_specs=P("row", "col"),
        check_vma=False,
    )
```

```python
import functools

import jax
import jax.numpy as jnp
from jax import lax
from jax.experimental import pallas as pl
from jax.experimental.pallas import tpu as pltpu
from jax.sharding import PartitionSpec as P

TILE = 16
BLOCK = 256
HEAD = 512
LANES = 128
GROUP = 8
CHUNK = 256
HIDDEN = 512
SET = 16
PASS = 256
PAYLOAD = 40
MIB = 1024 * 1024
F32 = jnp.float32
BF16 = jnp.bfloat16


def dot(a, b, precision=None):
    return jnp.dot(a, b, precision=precision, preferred_element_type=F32)


def dot_t(a, b):
    return lax.dot_general(a, b, (((1,), (1,)), ((), ())), preferred_element_type=F32)


def silu(v):
    half = 0.5 * v
    return half + half * jnp.tanh(half)


def hidden(feats, w_in, w_mid):
    one = silu(dot(feats, w_in)).astype(BF16)
    return silu(dot(one, w_mid)).astype(BF16)


def iota(shape, dim):
    return lax.broadcasted_iota(jnp.int32, shape, dim)


def head_rows(code_ref, recv_ref, w_in, w_mid, w_tile, head, sums):
    code = code_ref[...]
    slot = code // 32
    column = code % 32
    groups = code.shape[0]
    keep = slot < HEAD // TILE
    ones = jnp.where(keep, 1.0, 0.0).astype(F32)
    upto = jnp.where(iota((LANES, LANES), 0) <= iota((LANES, LANES), 1), 1.0, 0.0).astype(BF16)
    before = jnp.where(iota((groups, groups), 1) < iota((groups, groups), 0), 1.0, 0.0).astype(BF16)
    totals = jnp.broadcast_to(jnp.sum(ones, axis=1, keepdims=True), ones.shape)
    place = dot(ones.astype(BF16), upto) + dot(before, totals.astype(BF16)) - 1.0
    place = jnp.where(keep, place, -1.0)
    count = jnp.sum(ones).astype(jnp.int32)
    slot_f = slot.astype(F32)
    column_f = column.astype(F32)
    sums[...] = jnp.zeros_like(sums)

    def one_pass(step, carry):
        wanted = (iota((PASS, LANES), 0) + step * PASS).astype(F32)
        feats = jnp.zeros((PASS, LANES), F32)
        by_row = jnp.zeros((16, PASS), F32)
        by_col = jnp.zeros((PASS, 16), F32)
        which = iota((16, LANES), 0)
        for g in range(groups):
            pick = jnp.where(place[g : g + 1, :] == wanted, 1.0, 0.0).astype(BF16)
            block = recv_ref[g * 8 : (g + 1) * 8, 16:32, :].reshape(LANES, LANES)
            feats += dot(pick, block)
            where_to = jnp.where(
                which == 0, slot_f[g : g + 1, :], jnp.where(which == 1, column_f[g : g + 1, :], 0.0)
            ).astype(BF16)
            by_row += dot_t(where_to, pick)
            by_col += dot_t(pick, where_to)
        two = hidden(feats.astype(BF16), w_in[...], w_mid[...])
        col_c = by_col[:, 1:2].astype(jnp.int32)
        mask = iota((PASS, 2 * LANES), 1) % LANES // TILE == col_c % GROUP
        row_c = by_row[1:2, :].astype(jnp.int32)
        key = row_c // GROUP * (HEAD // TILE) + by_row[0:1, :].astype(jnp.int32)
        spread = jnp.where(iota((LANES, PASS), 0) == key, 1.0, 0.0).astype(F32)
        for j in range(TILE // 2):
            lanes = slice(j * 2 * LANES, (j + 1) * 2 * LANES)
            values = jnp.where(mask, dot(two, w_tile[:, lanes]), 0.0)
            sums[:, lanes] += dot(spread, values, lax.Precision.HIGHEST)
        return carry

    lax.fori_loop(0, (count + PASS - 1) // PASS, one_pass, 0)
    per = HEAD // TILE
    for a in range(TILE):
        for q in range(HEAD // LANES):
            head[pl.ds(q * HEAD + a, per, stride=TILE), :] = sums[
                q * per : (q + 1) * per, a * LANES : (a + 1) * LANES
            ]


def solve(head, dinv, corner, solved, solved_b):
    quarters = [head[q * HEAD : (q + 1) * HEAD, :] for q in range(HEAD // LANES)]
    rows = jnp.concatenate(quarters, axis=1)
    top = dot(dinv[0], rows[:BLOCK, :], lax.Precision.HIGHEST)
    top_b = top.astype(BF16)
    solved[:BLOCK, :] = top
    solved_b[:BLOCK, :] = top_b
    lost = dot(corner[:BLOCK, :], top_b[:LANES, :]) + dot(corner[BLOCK:, :], top_b[LANES:, :])
    rest = rows[BLOCK:, :] - lost
    low = dot(dinv[1], rest, lax.Precision.HIGHEST)
    solved[BLOCK:, :] = low
    solved_b[BLOCK:, :] = low.astype(BF16)


def some(bits):
    return bits != 0


def low_bit(bits):
    low = bits & -bits
    place = 0
    for width, mask in ((8, 0xFF00), (4, 0xF0F0), (2, 0xCCCC), (1, 0xAAAA)):
        place = place + jnp.where((low & mask) != 0, width, 0)
    return place


def hidden_kernel(code, recv, w_in, w_mid, w_tile, two, head, sums):
    def chunk(k, carry):
        peers = HIDDEN // SET
        feats = recv[pl.ds(pl.multiple_of(k * peers, peers), peers), 0:16, :].reshape(HIDDEN, LANES)
        two[pl.ds(pl.multiple_of(k * HIDDEN, HIDDEN), HIDDEN), :] = hidden(feats, w_in[...], w_mid[...])
        return carry

    head_rows(code, recv, w_in, w_mid, w_tile, head, sums)
    lax.fori_loop(0, two.shape[0] // HIDDEN, chunk, 0)


def assemble(dest, lost, clashes, two, lane_ref, w_tile, slab, tiles, early):
    peers = CHUNK // SET

    def clear(i, carry):
        slab[pl.ds(pl.multiple_of(i * 512, 512), 512), :] = jnp.zeros((512, LANES), F32)
        return carry

    lax.fori_loop(0, slab.shape[0] // 512, clear, 0, unroll=2)
    for copy in early:
        copy.wait()

    def chunk(k, carry):
        start = pl.multiple_of(k * peers, peers)
        rows = two[pl.ds(pl.multiple_of(k * CHUNK, CHUNK), CHUNK), :]
        lane = lane_ref[pl.ds(start, peers), :]
        lane = jnp.broadcast_to(lane[:, None, :], (peers, 16, 16)).reshape(CHUNK, 16)
        own = iota((CHUNK, 16), 0) % 16 == iota((CHUNK, 16), 1)
        lane = jnp.sum(jnp.where(own, lane, 0.0), axis=1, keepdims=True).astype(jnp.int32)
        mask = iota((CHUNK, LANES), 1) // TILE == lane
        for j in range(TILE // 2):
            pair = dot(rows, w_tile[:, j * 2 * LANES : (j + 1) * 2 * LANES])
            for i in range(2):
                tiles[pl.ds(2 * j + i, CHUNK, stride=TILE), :] = jnp.where(
                    mask, pair[:, i * LANES : (i + 1) * LANES], 0.0
                )

        def load(e):
            return tiles[pl.ds(pl.multiple_of(e * TILE, TILE), TILE), :]

        def place(i, inner):
            at = [pl.multiple_of(dest[k * CHUNK + i * SET + e], TILE) for e in range(SET)]
            sums = [slab[pl.ds(at[e], TILE), :] + load(i * SET + e) for e in range(SET)]
            for e in range(SET):
                slab[pl.ds(at[e], TILE), :] = sums[e]
            return inner

        def repair(bits):
            peer = low_bit(bits)

            def one(left):
                e = peer * SET + low_bit(left)
                at = pl.multiple_of(dest[k * CHUNK + e], TILE)
                slab[pl.ds(at, TILE), :] += load(e)
                return left & (left - 1)

            lax.while_loop(some, one, lost[k * peers + peer])
            return bits & (bits - 1)

        lax.fori_loop(0, CHUNK // SET, place, 0, unroll=4)
        lax.while_loop(some, repair, clashes[k])
        return carry

    lax.fori_loop(0, two.shape[0] // CHUNK, chunk, 0)


def final_kernel(count, *refs):
    place, dest, lost, clashes, two, lane, w_tile, head, dinv, corner = refs[:10]
    pieces = refs[10 : 10 + count]
    out, solved_b = refs[10 + count : 12 + count]
    slab, tiles, solved, panel, result, two_v, tile_v, in_sems, out_sems, sems = refs[12 + count :]
    total = out.shape[0]
    blocks = out_sems.shape[0]
    rows = total // blocks
    copies = [pltpu.make_async_copy(piece, panel.at[i], in_sems.at[i]) for i, piece in enumerate(pieces)]
    early = [pltpu.make_async_copy(two, two_v, sems.at[0]), pltpu.make_async_copy(w_tile, tile_v, sems.at[1])]
    for copy in early + copies:
        copy.start()
    solve(head, dinv, corner, solved, solved_b)
    assemble(dest, lost, clashes, two_v, lane, tile_v, slab, tiles, early)
    for copy in copies:
        copy.wait()

    def block(i):
        return pl.ds(pl.multiple_of(i * rows, rows), rows)

    def give(i):
        return pltpu.make_async_copy(result.at[block(i), :], out.at[block(place[i]), :], out_sems.at[i])

    def part(i, q):
        return slab[pl.ds(pl.multiple_of(q * total + place[i] * rows, rows), rows), :]

    def leave(i):
        @pl.when(jnp.logical_and(place[blocks] == 1, place[i] == 0))
        def _():
            result[block(i), :] = solved[...]

        give(i).start()

    def step(i, carry):
        for j in range(HEAD // (2 * LANES)):
            less = dot(panel[i], solved_b[:, j * 2 * LANES : (j + 1) * 2 * LANES])
            for q in (2 * j, 2 * j + 1):
                lanes = slice((q - 2 * j) * LANES, (q - 2 * j + 1) * LANES)
                result[block(i), q * LANES : (q + 1) * LANES] = part(i, q) - less[:, lanes]
        leave(i)
        return carry

    def plain(i, carry):
        for q in range(HEAD // LANES):
            result[block(i), q * LANES : (q + 1) * LANES] = part(i, q)
        leave(i)
        return carry

    lax.fori_loop(count, blocks, plain, 0)
    lax.fori_loop(0, count, step, 0)

    def finish(i, carry):
        give(i).wait()
        return carry

    lax.fori_loop(0, blocks, finish, 0)


def last_kernel(first, *refs):
    place, solved_b, before = refs[:3]
    count = place.shape[0] - 1 - first
    pieces = refs[3 : 3 + count]
    out, panel, result, in_sems, take_sems, out_sems = refs[3 + count :]
    rows = pieces[0].shape[0]

    def block(i):
        return pl.ds(pl.multiple_of(place[first + i] * rows, rows), rows)

    fetches = [pltpu.make_async_copy(pieces[i], panel.at[i], in_sems.at[i]) for i in range(count)]
    takes = [pltpu.make_async_copy(before.at[block(i), :], result.at[i], take_sems.at[i]) for i in range(count)]
    gives = [pltpu.make_async_copy(result.at[i], out.at[block(i), :], out_sems.at[i]) for i in range(count)]
    for copy in fetches + takes:
        copy.start()
    for i in range(count):
        fetches[i].wait()
        takes[i].wait()

        @pl.when(jnp.logical_not(jnp.logical_and(place[first + count] == 1, place[first + i] == 0)))
        def _():
            for j in range(HEAD // (2 * LANES)):
                lanes = slice(j * 2 * LANES, (j + 1) * 2 * LANES)
                result[i, :, lanes] -= dot(panel[i], solved_b[:, lanes])

        gives[i].start()
    for copy in gives:
        copy.wait()


def vmem():
    return pl.BlockSpec(memory_space=pltpu.VMEM)


def payload_kernel(feats, rows, cols, corner, out):
    peers = feats.shape[0]
    n_col = 16
    groups, per = rows.shape[0], peers // rows.shape[0]
    code = (rows[...] & 511) * 32 + (cols[...] & 31)
    high, low = (code >> 7).astype(F32), (code & 127).astype(F32)
    line = iota((8, LANES), 0)
    out[:, 0:16, :] = feats[...]
    for i in range(peers // n_col):
        out[i * n_col : (i + 1) * n_col, 16:32, :] = feats[:n_col, :, :]
    for g in range(groups):
        h = g % (n_col // per)
        block = jnp.where(line == 0, high[g : g + 1, :], low[g : g + 1, :])
        block = jnp.where(line == 2, high[h : h + 1, :], jnp.where(line == 3, low[h : h + 1, :], block))
        block = jnp.broadcast_to(block[None], (per, 8, LANES))
        slices = corner[g * per : (g + 1) * per, :, :].astype(F32)
        out[g * per : (g + 1) * per, 32:40, :] = jnp.where(line[None] < 4, block, slices).astype(BF16)


def along_x(value, by):
    return lax.ppermute(value, "col", [(z * 4 + x, z * 4 + (x + by) % 4) for z in range(4) for x in range(4)])


def along_z(value, by):
    return lax.ppermute(value, "col", [(z * 4 + x, (z + by) % 4 * 4 + x) for z in range(4) for x in range(4)])


def start_gather(own):
    got = {"own": own}
    got["left"], got["right"] = along_x(own, 1), along_x(own, -1)
    got["down"], got["up"] = along_z(own, 1), along_z(own, -1)
    return got


def together(got, *others):
    values = lax.optimization_barrier((*got.values(), *others))
    return dict(zip(got, values[: len(got)], strict=True)), *values[len(got) :]


def second_gather(near):
    got = {(0, 0): near["own"], (-1, 0): near["left"], (1, 0): near["right"], (0, -1): near["down"], (0, 1): near["up"]}
    got[1, 1] = along_x(got[0, 1], -1)
    got[1, -1] = along_z(got[1, 0], 1)
    got[-1, 1] = along_z(got[-1, 0], -1)
    got[-1, -1] = along_x(got[0, -1], 1)
    return got


def third_gather(got):
    got[2, 1] = along_x(got[1, 1], -1)
    got[-1, 2] = along_z(got[-1, 1], -1)
    got[2, 0] = along_x(got[-1, 0], 1)
    got[0, 2] = along_z(got[0, -1], 1)
    return got


def fourth_gather(got):
    got[2, -1] = along_x(got[1, -1], -1)
    got[1, 2] = along_z(got[1, 1], -1)
    got[2, 2] = along_x(got[-1, 2], 1)
    return got


def body(edge_feats, edge_rows, edge_cols, w_in, w_mid, w_out, cholesky_panel, diag_inverse):
    n_row = lax.axis_size("row")
    n_col = lax.axis_size("col")
    peers = n_row * n_col
    rows_dev = cholesky_panel.shape[0] * n_col
    slots = rows_dev // TILE
    got = start_gather(cholesky_panel)
    corner = cholesky_panel[BLOCK : 2 * BLOCK, :BLOCK]
    corner = jnp.concatenate([corner[:, :LANES], corner[:, LANES:]], axis=0).reshape(peers, 4, LANES)
    corner = jnp.pad(corner, ((0, 0), (4, 0), (0, 0)))

    feats = edge_feats.reshape(peers, 16, LANES)
    payload = pl.pallas_call(
        payload_kernel,
        out_shape=jax.ShapeDtypeStruct((peers, PAYLOAD, LANES), BF16),
        in_specs=[vmem()] * 4,
        out_specs=vmem(),
        compiler_params=pltpu.CompilerParams(vmem_limit_bytes=16 * MIB),
    )(feats, edge_rows.reshape(16, LANES), edge_cols.reshape(16, LANES), corner)
    payload, got = lax.optimization_barrier((payload, got))
    recv = lax.all_to_all(payload, ("row", "col"), 0, 0, tiled=True)
    corner = jnp.broadcast_to(recv[:1, 36:40, :], (peers, 4, LANES))
    corner = lax.all_to_all(corner, ("row", "col"), 0, 0, tiled=True).reshape(2 * BLOCK, LANES)
    own_lane = lax.axis_index("col") % GROUP * 16
    info = lax.dynamic_slice(recv, (0, 32, own_lane), (peers, 4, 16)).astype(jnp.int32)
    own = info[:, 0, :] * 128 + info[:, 1, :]
    own_row, own_col = own // 32, own % 32
    window = own_col // GROUP * rows_dev + own_row * TILE
    dest = window.reshape(-1)
    code = (info[:, 2, :] * 128 + info[:, 3, :]).reshape(-1, LANES)
    later = iota((SET, SET), 1) > iota((SET, SET), 0)
    same = (window[:, :, None] == window[:, None, :]) & later
    bit = 1 << jnp.arange(16, dtype=jnp.int32)
    lost = jnp.sum(jnp.where(jnp.any(same, axis=2), bit, 0), axis=1)
    clashes = jnp.sum(jnp.where(lost.reshape(-1, CHUNK // SET) != 0, bit, 0), axis=1)
    lane = (own_col % GROUP).astype(F32)

    source = iota((256, 16 * LANES), 0)
    target = iota((256, 16 * LANES), 1)
    repeat = (source == target // LANES * TILE + target % TILE).astype(BF16)
    w_tile = dot(w_out, repeat).astype(BF16)

    anywhere = pl.BlockSpec(memory_space=pl.ANY)
    smem = pl.BlockSpec(memory_space=pltpu.SMEM)
    got, recv = together(second_gather(got), recv)
    got = third_gather(got)
    two, head = pl.pallas_call(
        hidden_kernel,
        out_shape=(
            jax.ShapeDtypeStruct((16 * peers, w_mid.shape[1]), BF16),
            jax.ShapeDtypeStruct((HEAD * HEAD // LANES, LANES), F32),
        ),
        in_specs=[vmem()] * 5,
        out_specs=(vmem(), vmem()),
        scratch_shapes=[pltpu.VMEM((LANES, 16 * LANES), F32)],
        compiler_params=pltpu.CompilerParams(vmem_limit_bytes=20 * MIB),
        cost_estimate=pl.CostEstimate(flops=10_000_000_000, bytes_accessed=8_000_000, transcendentals=0),
    )(code, recv, w_in, w_mid, w_tile)
    got, two, head = together(got, two, head)
    ready = len(got)
    got = fourth_gather(got)
    me = lax.axis_index("col")
    x, z = me % 4, me // 4
    place = [(z + dz) % 4 * 4 + (x + dx) % 4 for dx, dz in got]
    place = jnp.stack(place + [(lax.axis_index("row") == 0).astype(jnp.int32)]).astype(jnp.int32)
    count = len(got)
    pieces = list(got.values())
    part, solved_b = pl.pallas_call(
        functools.partial(final_kernel, ready),
        out_shape=(
            jax.ShapeDtypeStruct((rows_dev, HEAD), F32),
            jax.ShapeDtypeStruct((HEAD, HEAD), BF16),
        ),
        in_specs=[smem] * 4 + [anywhere, vmem(), anywhere] + [vmem()] * 3 + [anywhere] * ready,
        out_specs=(anywhere, vmem()),
        scratch_shapes=[
            pltpu.VMEM((rows_dev * HEAD // LANES, LANES), F32),
            pltpu.VMEM((CHUNK * TILE, LANES), F32),
            pltpu.VMEM((HEAD, HEAD), F32),
            pltpu.VMEM((ready, *cholesky_panel.shape), BF16),
            pltpu.VMEM((rows_dev, HEAD), F32),
            pltpu.VMEM(two.shape, BF16),
            pltpu.VMEM(w_tile.shape, BF16),
            pltpu.SemaphoreType.DMA((ready,)),
            pltpu.SemaphoreType.DMA((count,)),
            pltpu.SemaphoreType.DMA((2,)),
        ],
        compiler_params=pltpu.CompilerParams(vmem_limit_bytes=56 * MIB),
        cost_estimate=pl.CostEstimate(flops=15_000_000_000, bytes_accessed=30_000_000, transcendentals=0),
    )(place, dest, lost, clashes, two, lane, w_tile, head, diag_inverse, corner, *pieces[:ready])
    left = count - ready
    return pl.pallas_call(
        functools.partial(last_kernel, ready),
        out_shape=jax.ShapeDtypeStruct((rows_dev, HEAD), F32),
        in_specs=[smem, vmem()] + [anywhere] * (1 + left),
        out_specs=anywhere,
        scratch_shapes=[
            pltpu.VMEM((left, *cholesky_panel.shape), BF16),
            pltpu.VMEM((left, cholesky_panel.shape[0], HEAD), F32),
            pltpu.SemaphoreType.DMA((left,)),
            pltpu.SemaphoreType.DMA((left,)),
            pltpu.SemaphoreType.DMA((left,)),
        ],
        input_output_aliases={2: 0},
        compiler_params=pltpu.CompilerParams(vmem_limit_bytes=16 * MIB),
        cost_estimate=pl.CostEstimate(flops=800_000_000, bytes_accessed=8_000_000, transcendentals=0),
    )(place, solved_b, part, *pieces[ready:])


def solution(mesh):
    return jax.shard_map(
        body,
        mesh=mesh,
        in_specs=(
            P(("row", "col"), None),
            P(("row", "col")),
            P(("row", "col")),
            P(),
            P(),
            P(),
            P(("row", "col"), None),
            P(),
        ),
        out_specs=P("row", "col"),
        check_vma=False,
    )
```
